512 devices in a mesh: inst: 16 (over z_lo, x, core), blk: 32 (over y, z_hi).
Axes of the slice: x: 4, y: 8, z: 8 (z_hi: 4, z_lo: 2; z = z_hi * 2 + z_lo), core: 2. Of those that a mesh axis runs over, the one named last changes fastest.
Arguments:
- state: float32 [16, 5, 16, 256, 256], P('inst', None, None, 'blk'), may hold values from -0.53 to 3.9, as said below
- multiples: int32 [7], replicated, may hold values from 1 to 4
Outputs:
- state_change: float32 [16, 5, 16, 256, 256], P('inst', None, None, 'blk')
The draws below stay inside these ranges and needn't reach their ends.
Inputs may be any that keep to these rules, and one draw needn't show every extreme that they name: `state`: density and pressure lie in 0.7 to 1.3, the axial velocity in 0.2 to 0.8 and the other two velocity components in -0.4 to 0.4; the last variable is the total energy p / 0.4 + rho (u u + v v + w w) / 2.
All inputs are finite; a program needn't handle non-finite values.
Results may differ from the reference program's by a relative error of at most 0.0003.
Values sent between devices are 32-bit elements; how exact they have to be, the bound alone decides.
A program may use at most 64 MiB of HBM per device.

```python
import math
import jax
import jax.numpy as jnp
from jax import lax

NT = 16
HARM = 7
NX = 16
NZ = 256
NY = 256


def draw_state(key, part):
    subkeys = jax.random.split(key, 5)
    layout = (NT, NX, NY, NZ)
    density = jax.random.uniform(subkeys[0], layout, jnp.float32, 0.7, 1.3)
    pressure = jax.random.uniform(subkeys[1], layout, jnp.float32, 0.7, 1.3)
    axial_speed = jax.random.uniform(subkeys[2], layout, jnp.float32, 0.2, 0.8)
    swirl_speed = jax.random.uniform(subkeys[3], layout, jnp.float32, -0.4, 0.4)
    radial_speed = jax.random.uniform(subkeys[4], layout, jnp.float32, -0.4, 0.4)
    energy = pressure / 0.4 + 0.5 * density * (axial_speed * axial_speed + swirl_speed * swirl_speed + radial_speed * radial_speed)
    return jnp.stack([density, density * axial_speed, density * swirl_speed, density * radial_speed, energy], axis=1)


def with_ends(values, stream_key, smallest, top_value):
    spot = [jax.random.randint(jax.random.fold_in(stream_key, axis), (), 0, length) for axis, length in enumerate(values.shape)]
    longest = values.shape.index(max(values.shape))
    neighbour = spot[:longest] + [(spot[longest] + 1) % values.shape[longest]] + spot[longest + 1:]
    return values.at[tuple(spot)].set(smallest).at[tuple(neighbour)].set(top_value)


def setup_inputs(seed: int = 0) -> dict:
    seeds = jax.random.split(jax.random.key(seed), 3)
    return {
        "state": draw_state(jax.random.fold_in(seeds[2], 71), 0),
        "multiples": with_ends(jax.random.randint(seeds[1], (HARM,), 1, 5), jax.random.fold_in(seeds[1], 1), 1, 4).astype(jnp.int32),
    }


heat_ratio = 1.4
segment_step = 0.05
smooth_weight = 0.5
base_rate = 0.5
diagonal_weight = 3.0

def limited(lower, upper):
    return jnp.maximum(0.0, jnp.minimum(lower, upper)) + jnp.minimum(0.0, jnp.maximum(lower, upper))

def take_part(array_in, offset, amount, along):
    return lax.slice_in_dim(array_in, offset, offset + amount, axis=along)

def primitive(conserved):
    density = conserved[:, 0]
    velocity = [conserved[:, 1] / density, conserved[:, 2] / density, conserved[:, 3] / density]
    kinetic = 0.5 * density * (velocity[0] * velocity[0] + velocity[1] * velocity[1] + velocity[2] * velocity[2])
    pressure = (heat_ratio - 1.0) * (conserved[:, 4] - kinetic)
    return [density] + velocity + [pressure]

def physical(states, normal):
    density = states[0]
    pressure = states[4]
    velocity = states[1:4]
    normal_speed = velocity[normal]
    energy = pressure / (heat_ratio - 1.0) + 0.5 * density * (velocity[0] * velocity[0] + velocity[1] * velocity[1] + velocity[2] * velocity[2])
    conserved = [density, density * velocity[0], density * velocity[1], density * velocity[2], energy]
    flux = [density * normal_speed]
    for member in range(3):
        momentum = density * normal_speed * velocity[member]
        if member == normal:
            momentum = momentum + pressure
        flux.append(momentum)
    flux.append((energy + pressure) * normal_speed)
    wave_speed = jnp.abs(normal_speed) + jnp.sqrt(heat_ratio * pressure / density)
    return (flux, conserved, wave_speed)

def divergence(states, along, normal):
    extent = states[0].shape[along]
    interior = extent - 4
    left_side = []
    right_side = []
    for component in states:
        differences = take_part(component, 1, extent - 1, along) - take_part(component, 0, extent - 1, along)
        slopes = limited(take_part(differences, 0, interior + 2, along), take_part(differences, 1, interior + 2, along))
        centres = take_part(component, 1, interior + 2, along)
        left_side.append(take_part(centres, 0, interior + 1, along) + 0.5 * take_part(slopes, 0, interior + 1, along))
        right_side.append(take_part(centres, 1, interior + 1, along) - 0.5 * take_part(slopes, 1, interior + 1, along))
    left_flux, left_cons, left_speed = physical(left_side, normal)
    right_flux, right_cons, right_speed = physical(right_side, normal)
    wave_speed = jnp.maximum(left_speed, right_speed)
    result = []
    for member in range(5):
        face_flux = 0.5 * (left_flux[member] + right_flux[member]) - 0.5 * wave_speed * (right_cons[member] - left_cons[member])
        result.append(take_part(face_flux, 1, interior, along) - take_part(face_flux, 0, interior, along))
    return result

def residual(extended):
    states = primitive(extended)
    inner = [component[:, :, 2:-2, :] for component in states]
    circum = divergence(states, 2, 1)
    axial = divergence([jnp.pad(component, ((0, 0), (2, 2), (0, 0), (0, 0)), mode='edge') for component in inner], 1, 0)
    radial = divergence([jnp.pad(component, ((0, 0), (0, 0), (0, 0), (2, 2)), mode='edge') for component in inner], 3, 2)
    return jnp.stack([axial[member] + circum[member] + radial[member] for member in range(5)], axis=1)

def wrap_pad(field):
    return jnp.pad(field, ((0, 0), (0, 0), (0, 0), (2, 2), (0, 0)), mode='wrap')

def two_sweeps(single):
    field = single[None]
    first_sweep = residual(wrap_pad(field))
    segmented = field - segment_step * first_sweep
    return residual(wrap_pad(segmented))[0]

def transform_tables(instances):
    indices = jnp.arange(instances, dtype=jnp.int32)
    harmonic = jnp.where(indices < 2, indices * (instances // 2), indices // 2)
    phases = harmonic[:, None] * indices[None, :] % instances
    angles = phases.astype(jnp.float32) * (2.0 * math.pi / instances)
    sine_rows = (indices % 2 == 1) & (indices >= 2)
    basis = jnp.where(sine_rows[:, None], jnp.sin(angles), jnp.cos(angles))
    weights = jnp.where(indices < 2, 1.0 / instances, 2.0 / instances).astype(jnp.float32)
    return (basis * weights[:, None], basis.T)

def pair_solve(right, frequency):
    cosine_part = right[:, 0]
    sine_part = right[:, 1]
    determinant = diagonal_weight * diagonal_weight + frequency * frequency
    return jnp.stack([(diagonal_weight * cosine_part - frequency * sine_part) / determinant, (diagonal_weight * sine_part + frequency * cosine_part) / determinant], axis=1)

def neighbours(correction):
    circum = jnp.roll(correction, 1, 4) + jnp.roll(correction, -1, 4)
    padded = jnp.pad(correction, ((0, 0), (0, 0), (0, 0), (0, 0), (0, 0), (1, 1)))
    return circum + (padded[:, :, :, :, :, :-2] + padded[:, :, :, :, :, 2:])

def reference(state, multiples):
    second_sweep = lax.map(two_sweeps, state)
    forward, inverse = transform_tables(NT)
    residual_hat = jnp.dot(forward, second_sweep.reshape(NT, -1), precision=lax.Precision.HIGHEST)
    state_hat = jnp.dot(forward, state.reshape(NT, -1), precision=lax.Precision.HIGHEST)
    layout = (NT // 2, 2) + state.shape[1:]
    residual_hat = residual_hat.reshape(layout)
    state_hat = state_hat.reshape(layout)
    frequency = jnp.concatenate([jnp.zeros((1,), jnp.float32), base_rate * multiples.astype(jnp.float32)]).reshape(NT // 2, 1, 1, 1, 1)
    source = jnp.stack([frequency * state_hat[:, 1], -frequency * state_hat[:, 0]], axis=1)
    right_hand = -(residual_hat + source)
    correction = pair_solve(right_hand, frequency)
    for repeat in range(3):
        correction = pair_solve(right_hand + smooth_weight * neighbours(correction), frequency)
    change = jnp.dot(inverse, correction.reshape(NT, -1), precision=lax.Precision.HIGHEST)
    return change.reshape(state.shape)
```

```python
import functools
import math

import jax
import jax.numpy as jnp
from jax import lax
from jax.experimental import pallas as pl
from jax.experimental.pallas import tpu as pltpu
from jax.sharding import PartitionSpec as P

NI = 16
NB = 32
MESH = pl.DeviceIdType.MESH
GROUPS = ((0,), (1,), (2,), (3,), (4,))
SOUND = math.sqrt(1.4)
C1 = math.cos(math.pi / 8)
C2 = math.sqrt(0.5)
C3 = math.sin(math.pi / 8)
OFFSETS = tuple(
    (z, x, c) for z in (1, 0) for x in (2, 1, 3, 0) for c in (1, 0) if (z, x, c) != (0, 0, 0)
)


def primitive(s):
    inv = 1.0 / s[0]
    u, v, w = s[1] * inv, s[2] * inv, s[3] * inv
    p = 0.4 * s[4] - 0.2 * (s[1] * u + s[2] * v + s[3] * w)
    return [s[0], u, v, w, p]


def face2(left, right, normal):
    def sound(q):
        t = q[0] * q[4]
        return (SOUND * q[4]) * lax.rsqrt(jnp.maximum(t, 1e-30))

    unl, unr = left[1 + normal], right[1 + normal]
    a = jnp.maximum(jnp.abs(unl) + sound(left), jnp.abs(unr) + sound(right))
    ml, mr = unl + a, unr - a
    gl, gr = left[0] * ml, right[0] * mr
    out = [gl + gr]
    kl = kr = None
    for m in range(3):
        fl, fr = gl * left[1 + m], gr * right[1 + m]
        flux = fl + fr
        if m == normal:
            flux = flux + (left[4] + right[4])
        out.append(flux)
        tl, tr = fl * left[1 + m], fr * right[1 + m]
        kl = tl if kl is None else kl + tl
        kr = tr if kr is None else kr + tr
    out.append(
        0.5 * (kl + kr)
        + (left[4] * (2.5 * ml + unl) + right[4] * (2.5 * mr + unr))
    )
    return out


def cell2(q, normal):
    un = q[1 + normal]
    half = q[0] * un
    g = half + half
    out = [g]
    for m in range(3):
        flux = g * q[1 + m]
        if m == normal:
            flux = flux + (q[4] + q[4])
        out.append(flux)
    out.append(half * (q[1] * q[1] + q[2] * q[2] + q[3] * q[3]) + 7.0 * q[4] * un)
    return out


def half_slope(a, b):
    return 0.5 * jnp.maximum(jnp.minimum(a, b), jnp.minimum(jnp.maximum(a, b), 0.0))


def shift_next(lo, hi, edge, axis):
    size = lo.shape[axis]
    last = lax.broadcasted_iota(jnp.int32, lo.shape, axis) == size - 1
    rl, rh = pltpu.roll(lo, size - 1, axis), pltpu.roll(hi, size - 1, axis)
    return jnp.where(last, rh, rl), jnp.where(last, edge, rh)


def shift_prev(lo, hi, edge, axis):
    first = lax.broadcasted_iota(jnp.int32, lo.shape, axis) == 0
    rl, rh = pltpu.roll(lo, 1, axis), pltpu.roll(hi, 1, axis)
    return jnp.where(first, edge, rl), jnp.where(first, rl, rh)


def line_div(lo, hi, normal, axis):
    left_lo, left_hi, right_lo, right_hi = [], [], [], []
    for v in range(5):
        a, b = lo[v], hi[v]
        na, nb = shift_next(a, b, b, axis)
        da, db = na - a, nb - b
        pa, pb = shift_prev(da, db, 0.0, axis)
        ha, hb = half_slope(pa, da), half_slope(pb, db)
        left_lo.append(a + ha)
        left_hi.append(b + hb)
        ra, rb = shift_next(a - ha, b - hb, b, axis)
        right_lo.append(ra)
        right_hi.append(rb)
    f_lo = face2(left_lo, right_lo, normal)
    f_hi = face2(left_hi, right_hi, normal)
    edge = cell2(lo, normal)
    out_lo, out_hi = [], []
    for v in range(5):
        a, b = shift_prev(f_lo[v], f_hi[v], edge[v], axis)
        out_lo.append(f_lo[v] - a)
        out_hi.append(f_hi[v] - b)
    return out_lo, out_hi


def axial_radial(prim, acc, r):
    q = [[prim[r, v, c] for v in range(5)] for c in range(4)]
    total = [None] * 4
    for c0, c1, normal, axis in ((0, 1, 2, 1), (2, 3, 2, 1), (0, 2, 0, 0), (1, 3, 0, 0)):
        lo, hi = line_div(q[c0], q[c1], normal, axis)
        for c, part in ((c0, lo), (c1, hi)):
            total[c] = part if total[c] is None else [s + t for s, t in zip(total[c], part)]
    for c in range(4):
        for v in range(5):
            acc[r, v, c] = total[c][v]


def column(prim, c, first, last, emit, before=None, after=None):
    lo = first - 2 if before is None else first - 1
    hi = last + 2 if after is None else last + 1
    w = {r: [prim[r, v, c] for v in range(5)] for r in range(lo, hi + 1)}
    d = {r: [w[r + 1][v] - w[r][v] for v in range(5)] for r in range(lo, hi)}
    h = {
        r: [half_slope(d[r - 1][v], d[r][v]) for v in range(5)] for r in range(lo + 1, hi)
    }

    def flux(r):
        return face2(
            [w[r][v] + h[r][v] for v in range(5)],
            [w[r + 1][v] - h[r + 1][v] for v in range(5)],
            1,
        )

    low = previous = flux(first - 1) if before is None else before
    for r in range(first, last + 1):
        face = after if r == last and after is not None else flux(r)
        emit(r, [face[v] - previous[v] for v in range(5)])
        previous = face
    return low, previous


def kernel(
    multiples, state, out,
    cons, prim, acc, edges, prim2, acc2,
    state_in, sweep_out, sweep_in, table, source,
    rhs, corr, last_corr, change,
    halo_send, halo_recv, state_send, state_recv, sweep_send, sweep_recv,
    rhs_send, rhs_recv, change_send, change_recv,
):
    me = lax.axis_index("inst")
    blk = lax.axis_index("blk")
    up, down = lax.rem(blk + 1, NB), lax.rem(blk + NB - 1, NB)
    my_core = lax.rem(me, 2)
    my_x = lax.rem(me // 2, 4)
    my_z = me // 8

    def peer(offset):
        z, x, c = offset
        return lax.rem(my_z + z, 2) * 8 + lax.rem(my_x + x, 4) * 2 + lax.rem(my_core + c, 2)

    barrier = pltpu.get_barrier_semaphore()
    for there in (up, down):
        pl.semaphore_signal(barrier, inc=1, device_id=(me, there), device_id_type=MESH)
    for offset in OFFSETS:
        pl.semaphore_signal(barrier, inc=1, device_id=(peer(offset), blk), device_id_type=MESH)

    for y in range(8):
        for c in range(4):
            rows = pl.ds((c // 2) * 64 + y, 8, stride=8)
            s = [state[v, c % 2, rows, :] for v in range(5)]
            q = primitive(s)
            for v in range(5):
                cons[y + 4, v, c] = s[v]
                prim[y + 4, v, c] = q[v]

    pl.semaphore_wait(barrier, NI - 1 + 2)

    def remote(source_ref, target_ref, send, recv, there):
        return pltpu.make_async_remote_copy(
            src_ref=source_ref, dst_ref=target_ref, send_sem=send, recv_sem=recv,
            device_id=there, device_id_type=MESH,
        )

    halos = []
    for k, (mine, theirs, there) in enumerate(
        ((4, 12, down), (10, 2, up), (6, 14, down), (8, 0, up))
    ):
        halos.append(
            remote(
                cons.at[pl.ds(mine, 2)], cons.at[pl.ds(theirs, 2)],
                halo_send.at[k], halo_recv.at[k], (me, there),
            )
        )
        halos[-1].start()

    for k in range(8):
        rate = 0.0 if k == 0 else 0.5 * multiples[k - 1].astype(jnp.float32)
        rate = jnp.full((8, 128), rate, jnp.float32)
        det = 9.0 + rate * rate
        table[0, k] = 3.0 / det
        table[1, k] = rate / det
        table[2, k] = rate * 0.125

    def own_axial_radial(r, carry):
        axial_radial(prim, acc, r)
        return carry

    lax.fori_loop(4, 12, own_axial_radial, 0)

    def halo_primitive(r):
        for c in range(4):
            q = primitive([cons[r, v, c] for v in range(5)])
            for v in range(5):
                prim[r, v, c] = q[v]

    halos[0].wait_recv()
    halos[1].wait_recv()
    for r in (2, 3, 12, 13):
        halo_primitive(r)

    def segment(c):
        def emit(r, diff):
            s = [cons[r, v, c] - 0.025 * (acc[r, v, c] + diff[v]) for v in range(5)]
            q = primitive(s)
            for v in range(5):
                prim2[r, v, c] = q[v]

        return emit

    def own_column(c, carry):
        low, high = column(prim, c, 4, 11, segment(c))
        for v in range(5):
            edges[0, v, c] = low[v]
            edges[1, v, c] = high[v]
        return carry

    lax.fori_loop(0, 4, own_column, 0)

    states = []
    for k, offset in enumerate(OFFSETS):
        t = peer(offset)
        states.append(
            remote(
                state.at[:, :, pl.ds(pl.multiple_of(8 * t, 8), 8), :], state_in.at[me],
                state_send.at[k], state_recv.at[k], (t, blk),
            )
        )
        states[-1].start()

    def sweep2_axial_radial(r, carry):
        axial_radial(prim2, acc2, r)
        return carry

    def halo_axial_radial(k, carry):
        axial_radial(prim, acc, k + 2 + 8 * (k // 2))
        return carry

    lax.fori_loop(0, 4, halo_axial_radial, 0)
    lax.fori_loop(4, 12, sweep2_axial_radial, 0)

    halos[2].wait_recv()
    halos[3].wait_recv()
    for r in (0, 1, 14, 15):
        halo_primitive(r)

    def halo_column(c, carry):
        column(prim, c, 2, 3, segment(c), after=[edges[0, v, c] for v in range(5)])
        column(prim, c, 12, 13, segment(c), before=[edges[1, v, c] for v in range(5)])
        return carry

    lax.fori_loop(0, 4, halo_column, 0)

    def sweep2_column(c, carry):
        xh, zh = c // 2, lax.rem(c, 2)

        def emit(r, diff):
            for v in range(5):
                rows = pl.ds(xh * 640 + v * 16 + zh * 8 + (r - 4), 8, stride=80)
                sweep_out[rows, :] = acc2[r, v, c] + diff[v]

        column(prim2, c, 4, 11, emit)
        return carry

    lax.fori_loop(0, 4, sweep2_column, 0)

    sweeps = []
    for g, group in enumerate(GROUPS):
        first, rows = 16 * group[0], 16 * len(group)
        sweeps.append([])
        for k, offset in enumerate(OFFSETS):
            t = peer(offset)
            sweeps[g].append(
                remote(
                    sweep_out.at[pl.ds(pl.multiple_of(80 * t + first, 8), rows)],
                    sweep_in.at[me, pl.ds(first, rows)],
                    sweep_send.at[g, k], sweep_recv.at[g, k], (t, blk),
                )
            )
            sweeps[g][-1].start()
    for v in range(5):
        for zh in range(2):
            state_in[me, v, zh] = state[v, zh, pl.ds(pl.multiple_of(8 * me, 8), 8), :]
    own = sweep_out[pl.ds(pl.multiple_of(80 * me, 8), 80), :]
    sweep_in[me] = own

    for copy in states:
        copy.wait_recv()

    def solve(k, a, b):
        alpha, beta = table[0, k], table[1, k]
        return alpha * a - beta * b, alpha * b + beta * a

    def source_of(v, carry):
        for zh in range(2):
            x = forward([state_in[n, v, zh] for n in range(NI)])
            for k in range(1, 8):
                scale = table[2, k]
                a, b = solve(k, -(scale * x[2 * k + 1]), scale * x[2 * k])
                source[v, zh, 2 * k] = a
                source[v, zh, 2 * k + 1] = b
        return carry

    lax.fori_loop(0, 5, source_of, 0)

    rhs_copies = []
    for g, group in enumerate(GROUPS):
        for copy in sweeps[g]:
            copy.wait_recv()

        def right_hand(v, carry):
            for zh in range(2):
                first = pl.multiple_of(v * 16 + zh * 8, 8)
                x = forward([sweep_in[n, pl.ds(first, 8), :] for n in range(NI)])
                for k in range(8):
                    if k == 0:
                        a, b = x[0] * (-1.0 / 96.0), x[1] * (-1.0 / 96.0)
                    else:
                        a, b = solve(k, x[2 * k] * (-0.0625), x[2 * k + 1] * (-0.0625))
                        a = a + source[v, zh, 2 * k]
                        b = b + source[v, zh, 2 * k + 1]
                    rhs[v, zh, pl.ds(3 * 16 + k, 8, stride=16), :] = a
                    rhs[v, zh, pl.ds(3 * 16 + 8 + k, 8, stride=16), :] = b
            return carry

        lax.fori_loop(group[0], group[-1] + 1, right_hand, 0)
        vs = pl.ds(group[0], len(group))
        pair = []
        for k, (mine, theirs, there) in enumerate(((3, 11, down), (8, 0, up))):
            pair.append(
                remote(
                    rhs.at[vs, :, pl.ds(16 * mine, 48), :], rhs.at[vs, :, pl.ds(16 * theirs, 48), :],
                    rhs_send.at[g, k], rhs_recv.at[g, k], (me, there),
                )
            )
            pair[-1].start()
        rhs_copies.append(pair)

    pair_index = lax.broadcasted_iota(jnp.int32, (8, 128), 0)
    rate = jnp.zeros((8, 128), jnp.float32)
    for k in range(1, 8):
        rate = jnp.where(pair_index == k, 0.5 * multiples[k - 1].astype(jnp.float32), rate)
    det = 9.0 + rate * rate
    alpha, beta = 1.5 / det, (0.5 * rate) / det

    changes = []
    for g, group in enumerate(GROUPS):
        for copy in rhs_copies[g]:
            copy.wait_recv()

        def smooth(v, carry):
            def at(ref, row, ab, zh, shift=0):
                return ref[v, zh, pl.ds(16 * (row - shift) + 8 * ab, 8), :]

            def step(src, dst, first, last, src_shift=0, dst_shift=0):
                for row in range(first, last + 1):
                    nb = []
                    for ab in range(2):
                        lo, hi = (at(src, row, ab, zh, src_shift) for zh in range(2))
                        nlo, nhi = shift_next(lo, hi, 0.0, 1)
                        plo, phi = shift_prev(lo, hi, 0.0, 1)
                        both = []
                        for zh, t in ((0, nlo + plo), (1, nhi + phi)):
                            y = at(src, row - 1, ab, zh, src_shift) + at(src, row + 1, ab, zh, src_shift)
                            both.append(y + t)
                        nb.append(both)
                    for zh in range(2):
                        a, b = nb[0][zh], nb[1][zh]
                        for ab, t in ((0, alpha * a - beta * b), (1, alpha * b + beta * a)):
                            dst[v, zh, pl.ds(16 * (row - dst_shift) + 8 * ab, 8), :] = (
                                at(rhs, row, ab, zh) + t
                            )

            step(rhs, corr.at[0], 1, 12)
            step(corr.at[0], corr.at[1], 2, 11)
            step(corr.at[1], last_corr, 3, 10, 0, 3)
            for zh in range(2):
                c = [
                    last_corr[v, zh, pl.ds(8 * ab + k, 8, stride=16), :]
                    for k in range(8)
                    for ab in range(2)
                ]
                x = backward(c)
                for n in range(NI):
                    change[n, v, zh] = x[n]
            return carry

        lax.fori_loop(group[0], group[-1] + 1, smooth, 0)
        vs = pl.ds(group[0], len(group))
        changes.append([])
        here = pl.ds(pl.multiple_of(8 * me, 8), 8)
        for k, offset in enumerate(OFFSETS):
            t = peer(offset)
            changes[g].append(
                remote(
                    change.at[t, vs], out.at[vs, :, here, :],
                    change_send.at[g, k], change_recv.at[g, k], (t, blk),
                )
            )
            changes[g][-1].start()
        for v in group:
            for zh in range(2):
                out[v, zh, here, :] = change[me, v, zh]

    for copies in [halos, states] + sweeps + rhs_copies:
        for copy in copies:
            copy.wait_send()
    for copies in changes:
        for copy in copies:
            copy.wait()


def forward(x):
    e = [x[n] + x[n + 8] for n in range(8)]
    o = [x[n] - x[n + 8] for n in range(8)]
    ee = [e[n] + e[n + 4] for n in range(4)]
    eo = [e[n] - e[n + 4] for n in range(4)]
    out = [None] * 16
    s, t = ee[0] + ee[2], ee[1] + ee[3]
    out[0], out[1] = s + t, s - t
    out[8], out[9] = ee[0] - ee[2], ee[1] - ee[3]
    s, t = C2 * (eo[1] - eo[3]), C2 * (eo[1] + eo[3])
    out[4], out[5] = eo[0] + s, t + eo[2]
    out[12], out[13] = eo[0] - s, t - eo[2]
    p = [o[n] - o[8 - n] for n in range(1, 4)]
    q = [o[n] + o[8 - n] for n in range(1, 4)]
    m = C2 * p[1]
    s, t = o[0] + m, o[0] - m
    y, z = C1 * p[0] + C3 * p[2], C3 * p[0] - C1 * p[2]
    out[2], out[14] = s + y, s - y
    out[6], out[10] = t + z, t - z
    m = C2 * q[1]
    s, t = m + o[4], m - o[4]
    y, z = C3 * q[0] + C1 * q[2], C1 * q[0] - C3 * q[2]
    out[3], out[15] = y + s, y - s
    out[7], out[11] = z + t, z - t
    return out


def backward(c):
    s, t = c[0] + c[1], c[0] - c[1]
    ee = [s + c[8], t + c[9], s - c[8], t - c[9]]
    y, z = C2 * (c[4] - c[12]), C2 * (c[5] + c[13])
    eo = [c[4] + c[12], z + y, c[5] - c[13], z - y]
    e = [ee[n] + eo[n] for n in range(4)] + [ee[n] - eo[n] for n in range(4)]
    s, d = c[2] + c[14], c[2] - c[14]
    t, g = c[6] + c[10], c[6] - c[10]
    p = [None, C1 * d + C3 * g, C2 * (s - t), C3 * d - C1 * g]
    o0 = s + t
    s, d = c[3] + c[15], c[3] - c[15]
    t, g = c[7] + c[11], c[7] - c[11]
    q = [None, C3 * s + C1 * t, C2 * (d + g), C1 * s - C3 * t]
    o4 = d - g
    o = [o0] + [q[n] + p[n] for n in range(1, 4)] + [o4]
    o += [q[n] - p[n] for n in (3, 2, 1)]
    return [e[n] + o[n] for n in range(8)] + [e[n] - o[n] for n in range(8)]


def body(state, multiples):
    f32 = jnp.float32
    tiles = lambda rows: pltpu.VMEM((rows, 5, 4, 8, 128), f32)
    peers = len(OFFSETS)
    groups = len(GROUPS)
    dma = pltpu.SemaphoreType.DMA
    halves = state.reshape(5, 128, 2, 128).transpose(0, 2, 1, 3)
    change = pl.pallas_call(
        kernel,
        out_shape=jax.ShapeDtypeStruct((5, 2, 128, 128), f32),
        in_specs=[
            pl.BlockSpec(memory_space=pltpu.SMEM),
            pl.BlockSpec(memory_space=pltpu.VMEM),
        ],
        out_specs=pl.BlockSpec(memory_space=pltpu.VMEM),
        scratch_shapes=[
            tiles(16), tiles(16), tiles(16),
            pltpu.VMEM((2, 5, 4, 8, 128), f32),
            tiles(16), tiles(16),
            pltpu.VMEM((NI, 5, 2, 8, 128), f32),
            pltpu.VMEM((NI * 80, 128), f32),
            pltpu.VMEM((NI, 80, 128), f32),
            pltpu.VMEM((3, 8, 8, 128), f32),
            pltpu.VMEM((5, 2, 16, 8, 128), f32),
            pltpu.VMEM((5, 2, 14 * 16, 128), f32),
            pltpu.VMEM((2, 5, 2, 14 * 16, 128), f32),
            pltpu.VMEM((5, 2, 8 * 16, 128), f32),
            pltpu.VMEM((NI, 5, 2, 8, 128), f32),
            dma((4,)), dma((4,)),
            dma((peers,)), dma((peers,)),
            dma((groups, peers)), dma((groups, peers)),
            dma((groups, 2)), dma((groups, 2)),
            dma((groups, peers)), dma((groups, peers)),
        ],
        compiler_params=pltpu.CompilerParams(
            collective_id=0, has_side_effects=True, vmem_limit_bytes=40 * 2**20
        ),
    )(multiples, halves)
    return change.transpose(0, 2, 1, 3).reshape(state.shape)


def solution(mesh):
    return jax.shard_map(
        body,
        mesh=mesh,
        in_specs=(P("inst", None, None, "blk", None), P()),
        out_specs=P("inst", None, None, "blk", None),
        check_vma=False,
    )
```

```python
import functools
import math

import jax
import jax.numpy as jnp
from jax import lax
from jax.experimental import pallas as pl
from jax.experimental.pallas import tpu as pltpu
from jax.sharding import PartitionSpec as P

NI = 16
NB = 32
MESH = pl.DeviceIdType.MESH
GROUPS = ((0,), (1,), (2,), (3,), (4,))
SOUND = math.sqrt(1.4)
C1 = math.cos(math.pi / 8)
C2 = math.sqrt(0.5)
C3 = math.sin(math.pi / 8)
OFFSETS = tuple(
    (z, x, c) for z in (1, 0) for x in (2, 1, 3, 0) for c in (1, 0) if (z, x, c) != (0, 0, 0)
)


def primitive(s):
    inv = 1.0 / s[0]
    u, v, w = s[1] * inv, s[2] * inv, s[3] * inv
    p = 0.4 * s[4] - 0.2 * (s[1] * u + s[2] * v + s[3] * w)
    return [s[0], u, v, w, p]


def face2(left, right, normal):
    def sound(q):
        t = q[0] * q[4]
        return (SOUND * q[4]) * lax.rsqrt(jnp.maximum(t, 1e-30))

    unl, unr = left[1 + normal], right[1 + normal]
    a = jnp.maximum(jnp.abs(unl) + sound(left), jnp.abs(unr) + sound(right))
    ml, mr = unl + a, unr - a
    gl, gr = left[0] * ml, right[0] * mr
    out = [gl + gr]
    kl = kr = None
    for m in range(3):
        fl, fr = gl * left[1 + m], gr * right[1 + m]
        flux = fl + fr
        if m == normal:
            flux = flux + (left[4] + right[4])
        out.append(flux)
        tl, tr = fl * left[1 + m], fr * right[1 + m]
        kl = tl if kl is None else kl + tl
        kr = tr if kr is None else kr + tr
    out.append(
        0.5 * (kl + kr)
        + (left[4] * (2.5 * ml + unl) + right[4] * (2.5 * mr + unr))
    )
    return out


def cell2(q, normal):
    un = q[1 + normal]
    half = q[0] * un
    g = half + half
    out = [g]
    for m in range(3):
        flux = g * q[1 + m]
        if m == normal:
            flux = flux + (q[4] + q[4])
        out.append(flux)
    out.append(half * (q[1] * q[1] + q[2] * q[2] + q[3] * q[3]) + 7.0 * q[4] * un)
    return out


def half_slope(a, b):
    return 0.5 * jnp.maximum(jnp.minimum(a, b), jnp.minimum(jnp.maximum(a, b), 0.0))


def shift_next(lo, hi, edge, axis):
    size = lo.shape[axis]
    last = lax.broadcasted_iota(jnp.int32, lo.shape, axis) == size - 1
    rl, rh = pltpu.roll(lo, size - 1, axis), pltpu.roll(hi, size - 1, axis)
    return jnp.where(last, rh, rl), jnp.where(last, edge, rh)


def shift_prev(lo, hi, edge, axis):
    first = lax.broadcasted_iota(jnp.int32, lo.shape, axis) == 0
    rl, rh = pltpu.roll(lo, 1, axis), pltpu.roll(hi, 1, axis)
    return jnp.where(first, edge, rl), jnp.where(first, rl, rh)


def line_div(lo, hi, normal, axis):
    left_lo, left_hi, right_lo, right_hi = [], [], [], []
    for v in range(5):
        a, b = lo[v], hi[v]
        na, nb = shift_next(a, b, b, axis)
        da, db = na - a, nb - b
        pa, pb = shift_prev(da, db, 0.0, axis)
        ha, hb = half_slope(pa, da), half_slope(pb, db)
        left_lo.append(a + ha)
        left_hi.append(b + hb)
        ra, rb = shift_next(a - ha, b - hb, b, axis)
        right_lo.append(ra)
        right_hi.append(rb)
    f_lo = face2(left_lo, right_lo, normal)
    f_hi = face2(left_hi, right_hi, normal)
    edge = cell2(lo, normal)
    out_lo, out_hi = [], []
    for v in range(5):
        a, b = shift_prev(f_lo[v], f_hi[v], edge[v], axis)
        out_lo.append(f_lo[v] - a)
        out_hi.append(f_hi[v] - b)
    return out_lo, out_hi


def axial_radial(prim, acc, r):
    q = [[prim[r, v, c] for v in range(5)] for c in range(4)]
    total = [None] * 4
    for c0, c1, normal, axis in ((0, 1, 2, 1), (2, 3, 2, 1), (0, 2, 0, 0), (1, 3, 0, 0)):
        lo, hi = line_div(q[c0], q[c1], normal, axis)
        for c, part in ((c0, lo), (c1, hi)):
            total[c] = part if total[c] is None else [s + t for s, t in zip(total[c], part)]
    for c in range(4):
        for v in range(5):
            acc[r, v, c] = total[c][v]


def column(prim, c, first, last, emit, before=None, after=None):
    lo = first - 2 if before is None else first - 1
    hi = last + 2 if after is None else last + 1
    w = {r: [prim[r, v, c] for v in range(5)] for r in range(lo, hi + 1)}
    d = {r: [w[r + 1][v] - w[r][v] for v in range(5)] for r in range(lo, hi)}
    h = {
        r: [half_slope(d[r - 1][v], d[r][v]) for v in range(5)] for r in range(lo + 1, hi)
    }

    def flux(r):
        return face2(
            [w[r][v] + h[r][v] for v in range(5)],
            [w[r + 1][v] - h[r + 1][v] for v in range(5)],
            1,
        )

    low = previous = flux(first - 1) if before is None else before
    for r in range(first, last + 1):
        face = after if r == last and after is not None else flux(r)
        emit(r, [face[v] - previous[v] for v in range(5)])
        previous = face
    return low, previous


def kernel(
    multiples_hbm, state_hbm, out,
    multiples, state, cons, prim, acc, edges, prim2, acc2,
    state_out, state_in, relay_out, sweep_out, sweep_in, table, source,
    rhs, corr, last_corr, change,
    load_sem, halo_send, halo_recv, state_send, state_recv, relay_send, relay_recv, sweep_send, sweep_recv,
    rhs_send, rhs_recv, change_send, change_recv,
):
    me = lax.axis_index("inst")
    blk = lax.axis_index("blk")
    up, down = lax.rem(blk + 1, NB), lax.rem(blk + NB - 1, NB)
    my_core = lax.rem(me, 2)
    my_x = lax.rem(me // 2, 4)
    my_z = me // 8

    def peer(offset):
        z, x, c = offset
        return lax.rem(my_z + z, 2) * 8 + lax.rem(my_x + x, 4) * 2 + lax.rem(my_core + c, 2)

    relay_blk = lax.rem(blk + NB - 1 + 2 * my_z, NB)
    other_z = 1 - my_z

    barrier = pltpu.get_barrier_semaphore()
    for there in (up, down):
        pl.semaphore_signal(barrier, inc=1, device_id=(me, there), device_id_type=MESH)
    for offset in OFFSETS:
        pl.semaphore_signal(barrier, inc=1, device_id=(peer(offset), blk), device_id_type=MESH)
        if offset[0] == 1:
            pl.semaphore_signal(
                barrier, inc=1, device_id=(peer(offset), relay_blk), device_id_type=MESH
            )

    loads = [
        pltpu.make_async_copy(
            state_hbm.at[:, :, pl.ds(128 * zh, 128)], state.at[zh], load_sem.at[zh]
        )
        for zh in range(2)
    ]
    loads.append(pltpu.make_async_copy(multiples_hbm, multiples, load_sem.at[2]))
    for copy in loads:
        copy.start()
    for copy in loads:
        copy.wait()

    for y in range(8):
        for c in range(4):
            rows = pl.ds((c // 2) * 64 + y, 8, stride=8)
            s = [state[c % 2, v, rows, :] for v in range(5)]
            q = primitive(s)
            for v in range(5):
                cons[y + 4, v, c] = s[v]
                prim[y + 4, v, c] = q[v]
                row = (c // 2) * 640 + (y // 4) * 40 + v * 8 + (c % 2) * 4 + y % 4
                state_out[pl.ds(row, 8, stride=80), :] = s[v]

    pl.semaphore_wait(barrier, NI - 1 + 2 + 8)

    def remote(source_ref, target_ref, send, recv, there):
        return pltpu.make_async_remote_copy(
            src_ref=source_ref, dst_ref=target_ref, send_sem=send, recv_sem=recv,
            device_id=there, device_id_type=MESH,
        )

    halos = []
    for k, (mine, theirs, there) in enumerate(
        ((4, 12, down), (10, 2, up), (6, 14, down), (8, 0, up))
    ):
        halos.append(
            remote(
                cons.at[pl.ds(mine, 2)], cons.at[pl.ds(theirs, 2)],
                halo_send.at[k], halo_recv.at[k], (me, there),
            )
        )
        halos[-1].start()

    for k in range(8):
        rate = 0.0 if k == 0 else 0.5 * multiples[k - 1].astype(jnp.float32)
        rate = jnp.full((8, 128), rate, jnp.float32)
        det = 9.0 + rate * rate
        table[0, k] = 3.0 / det
        table[1, k] = rate / det
        table[2, k] = rate * 0.125

    def own_axial_radial(r, carry):
        axial_radial(prim, acc, r)
        return carry

    lax.fori_loop(4, 12, own_axial_radial, 0)

    def halo_primitive(r):
        for c in range(4):
            q = primitive([cons[r, v, c] for v in range(5)])
            for v in range(5):
                prim[r, v, c] = q[v]

    halos[0].wait_recv()
    halos[1].wait_recv()
    for r in (2, 3, 12, 13):
        halo_primitive(r)

    def segment(c):
        def emit(r, diff):
            s = [cons[r, v, c] - 0.025 * (acc[r, v, c] + diff[v]) for v in range(5)]
            q = primitive(s)
            for v in range(5):
                prim2[r, v, c] = q[v]

        return emit

    def own_column(c, carry):
        low, high = column(prim, c, 4, 11, segment(c))
        for v in range(5):
            edges[0, v, c] = low[v]
            edges[1, v, c] = high[v]
        return carry

    lax.fori_loop(0, 4, own_column, 0)

    def sweep2_axial_radial(r, carry):
        axial_radial(prim2, acc2, r)
        return carry

    def halo_axial_radial(k, carry):
        axial_radial(prim, acc, k + 2 + 8 * (k // 2))
        return carry

    lax.fori_loop(0, 4, halo_axial_radial, 0)
    lax.fori_loop(4, 12, sweep2_axial_radial, 0)

    states = []
    for k, offset in enumerate(OFFSETS):
        t = peer(offset)
        first, rows = (0, 80) if offset[0] == 0 else (pl.multiple_of(40 * my_z, 8), 40)
        states.append(
            remote(
                state_out.at[pl.ds(pl.multiple_of(80 * t + first, 8), rows)],
                state_in.at[me, pl.ds(first, rows)],
                state_send.at[k], state_recv.at[k], (t, blk),
            )
        )
        states[-1].start()
    own = state_out[pl.ds(pl.multiple_of(80 * me, 8), 80), :]
    state_in[me] = own

    halos[2].wait_recv()
    halos[3].wait_recv()
    for y in range(4):
        for v in range(5):
            for zh in range(2):
                relay_out[pl.ds(v * 8 + zh * 4 + y, 8, stride=40), :] = cons[
                    12 * my_z + y, v, 2 * other_z + zh
                ]
    for r in (0, 1, 14, 15):
        halo_primitive(r)

    def halo_column(c, carry):
        column(prim, c, 2, 3, segment(c), after=[edges[0, v, c] for v in range(5)])
        column(prim, c, 12, 13, segment(c), before=[edges[1, v, c] for v in range(5)])
        return carry

    lax.fori_loop(0, 4, halo_column, 0)

    def sweep2_column(c, carry):
        xh, zh = c // 2, lax.rem(c, 2)

        def emit(r, diff):
            for v in range(5):
                rows = pl.ds(xh * 640 + v * 16 + zh * 8 + (r - 4), 8, stride=80)
                sweep_out[rows, :] = acc2[r, v, c] + diff[v]

        column(prim2, c, 4, 11, emit)
        return carry

    lax.fori_loop(0, 4, sweep2_column, 0)

    sweeps = []
    for g, group in enumerate(GROUPS):
        first, rows = 16 * group[0], 16 * len(group)
        sweeps.append([])
        for k, offset in enumerate(OFFSETS):
            t = peer(offset)
            sweeps[g].append(
                remote(
                    sweep_out.at[pl.ds(pl.multiple_of(80 * t + first, 8), rows)],
                    sweep_in.at[me, pl.ds(first, rows)],
                    sweep_send.at[g, k], sweep_recv.at[g, k], (t, blk),
                )
            )
            sweeps[g][-1].start()
    own = sweep_out[pl.ds(pl.multiple_of(80 * me, 8), 80), :]
    sweep_in[me] = own

    relays = []
    for k, offset in enumerate(OFFSETS):
        if offset[0] == 1:
            t = peer(offset)
            relays.append(
                remote(
                    relay_out.at[pl.ds(pl.multiple_of(40 * (t - 8 * other_z), 8), 40)],
                    state_in.at[me, pl.ds(pl.multiple_of(40 * other_z, 8), 40)],
                    relay_send.at[k], relay_recv.at[k], (t, relay_blk),
                )
            )
            relays[-1].start()

    for copy in states + relays:
        copy.wait_recv()

    def solve(k, a, b):
        alpha, beta = table[0, k], table[1, k]
        return alpha * a - beta * b, alpha * b + beta * a

    def source_of(v, carry):
        for half in range(2):
            first = pl.multiple_of(v * 8 + half * 40, 8)
            x = forward([state_in[n, pl.ds(first, 8), :] for n in range(NI)])
            for k in range(1, 8):
                scale = table[2, k]
                a, b = solve(k, -(scale * x[2 * k + 1]), scale * x[2 * k])
                for zh in range(2):
                    rows = pl.ds(half * 4, 4)
                    source[v, zh, 2 * k, rows, :] = a[zh * 4 : zh * 4 + 4]
                    source[v, zh, 2 * k + 1, rows, :] = b[zh * 4 : zh * 4 + 4]
        return carry

    lax.fori_loop(0, 5, source_of, 0)

    rhs_copies = []
    for g, group in enumerate(GROUPS):
        for copy in sweeps[g]:
            copy.wait_recv()

        def right_hand(v, carry):
            for zh in range(2):
                first = pl.multiple_of(v * 16 + zh * 8, 8)
                x = forward([sweep_in[n, pl.ds(first, 8), :] for n in range(NI)])
                for k in range(8):
                    if k == 0:
                        a, b = x[0] * (-1.0 / 96.0), x[1] * (-1.0 / 96.0)
                    else:
                        a, b = solve(k, x[2 * k] * (-0.0625), x[2 * k + 1] * (-0.0625))
                        a = a + source[v, zh, 2 * k]
                        b = b + source[v, zh, 2 * k + 1]
                    rhs[v, zh, pl.ds(3 * 16 + k, 8, stride=16), :] = a
                    rhs[v, zh, pl.ds(3 * 16 + 8 + k, 8, stride=16), :] = b
            return carry

        lax.fori_loop(group[0], group[-1] + 1, right_hand, 0)
        vs = pl.ds(group[0], len(group))
        pair = []
        for k, (mine, theirs, there) in enumerate(((3, 11, down), (8, 0, up))):
            pair.append(
                remote(
                    rhs.at[vs, :, pl.ds(16 * mine, 48), :], rhs.at[vs, :, pl.ds(16 * theirs, 48), :],
                    rhs_send.at[g, k], rhs_recv.at[g, k], (me, there),
                )
            )
            pair[-1].start()
        rhs_copies.append(pair)

    pair_index = lax.broadcasted_iota(jnp.int32, (8, 128), 0)
    rate = jnp.zeros((8, 128), jnp.float32)
    for k in range(1, 8):
        rate = jnp.where(pair_index == k, 0.5 * multiples[k - 1].astype(jnp.float32), rate)
    det = 9.0 + rate * rate
    alpha, beta = 1.5 / det, (0.5 * rate) / det

    changes = []
    for g, group in enumerate(GROUPS):
        for copy in rhs_copies[g]:
            copy.wait_recv()

        def smooth(v, carry):
            def at(ref, row, ab, zh, shift=0):
                return ref[v, zh, pl.ds(16 * (row - shift) + 8 * ab, 8), :]

            def step(src, dst, first, last, src_shift=0, dst_shift=0):
                for row in range(first, last + 1):
                    nb = []
                    for ab in range(2):
                        lo, hi = (at(src, row, ab, zh, src_shift) for zh in range(2))
                        nlo, nhi = shift_next(lo, hi, 0.0, 1)
                        plo, phi = shift_prev(lo, hi, 0.0, 1)
                        both = []
                        for zh, t in ((0, nlo + plo), (1, nhi + phi)):
                            y = at(src, row - 1, ab, zh, src_shift) + at(src, row + 1, ab, zh, src_shift)
                            both.append(y + t)
                        nb.append(both)
                    for zh in range(2):
                        a, b = nb[0][zh], nb[1][zh]
                        for ab, t in ((0, alpha * a - beta * b), (1, alpha * b + beta * a)):
                            dst[v, zh, pl.ds(16 * (row - dst_shift) + 8 * ab, 8), :] = (
                                at(rhs, row, ab, zh) + t
                            )

            step(rhs, corr.at[0], 1, 12)
            step(corr.at[0], corr.at[1], 2, 11)
            step(corr.at[1], last_corr, 3, 10, 0, 3)
            for zh in range(2):
                c = [
                    last_corr[v, zh, pl.ds(8 * ab + k, 8, stride=16), :]
                    for k in range(8)
                    for ab in range(2)
                ]
                x = backward(c)
                for n in range(NI):
                    change[n, v, :, pl.ds(128 * zh, 128)] = x[n]
            return carry

        lax.fori_loop(group[0], group[-1] + 1, smooth, 0)
        vs = pl.ds(group[0], len(group))
        changes.append([])
        here = pl.ds(pl.multiple_of(8 * me, 8), 8)
        for k, offset in enumerate(OFFSETS):
            t = peer(offset)
            changes[g].append(
                remote(
                    change.at[t, vs], out.at[vs, here, :],
                    change_send.at[g, k], change_recv.at[g, k], (t, blk),
                )
            )
            changes[g][-1].start()
        for v in group:
            out[v, here, :] = change[me, v]

    for copies in [halos, states, relays] + sweeps + rhs_copies:
        for copy in copies:
            copy.wait_send()
    for copies in changes:
        for copy in copies:
            copy.wait()


def forward(x):
    e = [x[n] + x[n + 8] for n in range(8)]
    o = [x[n] - x[n + 8] for n in range(8)]
    ee = [e[n] + e[n + 4] for n in range(4)]
    eo = [e[n] - e[n + 4] for n in range(4)]
    out = [None] * 16
    s, t = ee[0] + ee[2], ee[1] + ee[3]
    out[0], out[1] = s + t, s - t
    out[8], out[9] = ee[0] - ee[2], ee[1] - ee[3]
    s, t = C2 * (eo[1] - eo[3]), C2 * (eo[1] + eo[3])
    out[4], out[5] = eo[0] + s, t + eo[2]
    out[12], out[13] = eo[0] - s, t - eo[2]
    p = [o[n] - o[8 - n] for n in range(1, 4)]
    q = [o[n] + o[8 - n] for n in range(1, 4)]
    m = C2 * p[1]
    s, t = o[0] + m, o[0] - m
    y, z = C1 * p[0] + C3 * p[2], C3 * p[0] - C1 * p[2]
    out[2], out[14] = s + y, s - y
    out[6], out[10] = t + z, t - z
    m = C2 * q[1]
    s, t = m + o[4], m - o[4]
    y, z = C3 * q[0] + C1 * q[2], C1 * q[0] - C3 * q[2]
    out[3], out[15] = y + s, y - s
    out[7], out[11] = z + t, z - t
    return out


def backward(c):
    s, t = c[0] + c[1], c[0] - c[1]
    ee = [s + c[8], t + c[9], s - c[8], t - c[9]]
    y, z = C2 * (c[4] - c[12]), C2 * (c[5] + c[13])
    eo = [c[4] + c[12], z + y, c[5] - c[13], z - y]
    e = [ee[n] + eo[n] for n in range(4)] + [ee[n] - eo[n] for n in range(4)]
    s, d = c[2] + c[14], c[2] - c[14]
    t, g = c[6] + c[10], c[6] - c[10]
    p = [None, C1 * d + C3 * g, C2 * (s - t), C3 * d - C1 * g]
    o0 = s + t
    s, d = c[3] + c[15], c[3] - c[15]
    t, g = c[7] + c[11], c[7] - c[11]
    q = [None, C3 * s + C1 * t, C2 * (d + g), C1 * s - C3 * t]
    o4 = d - g
    o = [o0] + [q[n] + p[n] for n in range(1, 4)] + [o4]
    o += [q[n] - p[n] for n in (3, 2, 1)]
    return [e[n] + o[n] for n in range(8)] + [e[n] - o[n] for n in range(8)]


def body(state, multiples):
    f32 = jnp.float32
    tiles = lambda rows: pltpu.VMEM((rows, 5, 4, 8, 128), f32)
    peers = len(OFFSETS)
    groups = len(GROUPS)
    dma = pltpu.SemaphoreType.DMA
    change = pl.pallas_call(
        kernel,
        out_shape=jax.ShapeDtypeStruct((5, 128, 256), f32),
        in_specs=[
            pl.BlockSpec(memory_space=pl.ANY),
            pl.BlockSpec(memory_space=pl.ANY),
        ],
        out_specs=pl.BlockSpec(memory_space=pltpu.VMEM),
        scratch_shapes=[
            pltpu.SMEM((7,), jnp.int32),
            pltpu.VMEM((2, 5, 128, 128), f32),
            tiles(16), tiles(16), tiles(16),
            pltpu.VMEM((2, 5, 4, 8, 128), f32),
            tiles(16), tiles(16),
            pltpu.VMEM((NI * 80, 128), f32),
            pltpu.VMEM((NI, 80, 128), f32),
            pltpu.VMEM((8 * 40, 128), f32),
            pltpu.VMEM((NI * 80, 128), f32),
            pltpu.VMEM((NI, 80, 128), f32),
            pltpu.VMEM((3, 8, 8, 128), f32),
            pltpu.VMEM((5, 2, 16, 8, 128), f32),
            pltpu.VMEM((5, 2, 14 * 16, 128), f32),
            pltpu.VMEM((2, 5, 2, 14 * 16, 128), f32),
            pltpu.VMEM((5, 2, 8 * 16, 128), f32),
            pltpu.VMEM((NI, 5, 8, 256), f32),
            dma((3,)),
            dma((4,)), dma((4,)),
            dma((peers,)), dma((peers,)),
            dma((8,)), dma((8,)),
            dma((groups, peers)), dma((groups, peers)),
            dma((groups, 2)), dma((groups, 2)),
            dma((groups, peers)), dma((groups, peers)),
        ],
        compiler_params=pltpu.CompilerParams(
            collective_id=0, has_side_effects=True, vmem_limit_bytes=40 * 2**20
        ),
    )(multiples, state.reshape(5, 128, 256))
    return change.reshape(state.shape)


def solution(mesh):
    return jax.shard_map(
        body,
        mesh=mesh,
        in_specs=(P("inst", None, None, "blk", None), P()),
        out_specs=P("inst", None, None, "blk", None),
        check_vma=False,
    )
```

```python
import functools
import math

import jax
import jax.numpy as jnp
from jax import lax
from jax.experimental import pallas as pl
from jax.experimental.pallas import tpu as pltpu
from jax.sharding import PartitionSpec as P

NI = 16
NB = 32
MESH = pl.DeviceIdType.MESH
GROUPS = ((0,), (1,), (2,), (3,), (4,))
SOUND = math.sqrt(1.4)
C1 = math.cos(math.pi / 8)
C2 = math.sqrt(0.5)
C3 = math.sin(math.pi / 8)
OFFSETS = tuple(
    (z, x, c) for z in (1, 0) for x in (2, 1, 3, 0) for c in (1, 0) if (z, x, c) != (0, 0, 0)
)


def primitive(s):
    inv = 1.0 / s[0]
    u, v, w = s[1] * inv, s[2] * inv, s[3] * inv
    p = 0.4 * s[4] - 0.2 * (s[1] * u + s[2] * v + s[3] * w)
    return [s[0], u, v, w, p]


def face2(left, right, normal):
    def sound(q):
        t = q[0] * q[4]
        return (SOUND * q[4]) * lax.rsqrt(jnp.maximum(t, 1e-30))

    unl, unr = left[1 + normal], right[1 + normal]
    a = jnp.maximum(jnp.abs(unl) + sound(left), jnp.abs(unr) + sound(right))
    ml, mr = unl + a, unr - a
    gl, gr = left[0] * ml, right[0] * mr
    out = [gl + gr]
    kl = kr = None
    for m in range(3):
        fl, fr = gl * left[1 + m], gr * right[1 + m]
        flux = fl + fr
        if m == normal:
            flux = flux + (left[4] + right[4])
        out.append(flux)
        tl, tr = fl * left[1 + m], fr * right[1 + m]
        kl = tl if kl is None else kl + tl
        kr = tr if kr is None else kr + tr
    out.append(
        0.5 * (kl + kr)
        + (left[4] * (2.5 * ml + unl) + right[4] * (2.5 * mr + unr))
    )
    return out


def cell2(q, normal):
    un = q[1 + normal]
    half = q[0] * un
    g = half + half
    out = [g]
    for m in range(3):
        flux = g * q[1 + m]
        if m == normal:
            flux = flux + (q[4] + q[4])
        out.append(flux)
    out.append(half * (q[1] * q[1] + q[2] * q[2] + q[3] * q[3]) + 7.0 * q[4] * un)
    return out


def half_slope(a, b):
    return 0.5 * jnp.maximum(jnp.minimum(a, b), jnp.minimum(jnp.maximum(a, b), 0.0))


def shift_next(lo, hi, edge, axis):
    size = lo.shape[axis]
    last = lax.broadcasted_iota(jnp.int32, lo.shape, axis) == size - 1
    rl, rh = pltpu.roll(lo, size - 1, axis), pltpu.roll(hi, size - 1, axis)
    return jnp.where(last, rh, rl), jnp.where(last, edge, rh)


def shift_prev(lo, hi, edge, axis):
    first = lax.broadcasted_iota(jnp.int32, lo.shape, axis) == 0
    rl, rh = pltpu.roll(lo, 1, axis), pltpu.roll(hi, 1, axis)
    return jnp.where(first, edge, rl), jnp.where(first, rl, rh)


def line_div(lo, hi, normal, axis):
    left_lo, left_hi, right_lo, right_hi = [], [], [], []
    for v in range(5):
        a, b = lo[v], hi[v]
        na, nb = shift_next(a, b, b, axis)
        da, db = na - a, nb - b
        pa, pb = shift_prev(da, db, 0.0, axis)
        ha, hb = half_slope(pa, da), half_slope(pb, db)
        left_lo.append(a + ha)
        left_hi.append(b + hb)
        ra, rb = shift_next(a - ha, b - hb, b, axis)
        right_lo.append(ra)
        right_hi.append(rb)
    f_lo = face2(left_lo, right_lo, normal)
    f_hi = face2(left_hi, right_hi, normal)
    edge = cell2(lo, normal)
    out_lo, out_hi = [], []
    for v in range(5):
        a, b = shift_prev(f_lo[v], f_hi[v], edge[v], axis)
        out_lo.append(f_lo[v] - a)
        out_hi.append(f_hi[v] - b)
    return out_lo, out_hi


def axial_radial(prim, acc, r):
    q = [[prim[r, v, c] for v in range(5)] for c in range(4)]
    total = [None] * 4
    for c0, c1, normal, axis in ((0, 1, 2, 1), (2, 3, 2, 1), (0, 2, 0, 0), (1, 3, 0, 0)):
        lo, hi = line_div(q[c0], q[c1], normal, axis)
        for c, part in ((c0, lo), (c1, hi)):
            total[c] = part if total[c] is None else [s + t for s, t in zip(total[c], part)]
    for c in range(4):
        for v in range(5):
            acc[r, v, c] = total[c][v]


def column(prim, c, first, last, emit, before=None, after=None):
    lo = first - 2 if before is None else first - 1
    hi = last + 2 if after is None else last + 1
    w = {r: [prim[r, v, c] for v in range(5)] for r in range(lo, hi + 1)}
    d = {r: [w[r + 1][v] - w[r][v] for v in range(5)] for r in range(lo, hi)}
    h = {
        r: [half_slope(d[r - 1][v], d[r][v]) for v in range(5)] for r in range(lo + 1, hi)
    }

    def flux(r):
        return face2(
            [w[r][v] + h[r][v] for v in range(5)],
            [w[r + 1][v] - h[r + 1][v] for v in range(5)],
            1,
        )

    low = previous = flux(first - 1) if before is None else before
    for r in range(first, last + 1):
        face = after if r == last and after is not None else flux(r)
        emit(r, [face[v] - previous[v] for v in range(5)])
        previous = face
    return low, previous


def kernel(
    multiples_hbm, state_hbm, out,
    multiples, state, cons, prim, acc, edges, prim2, acc2,
    state_out, state_in, relay_out, sweep_out, sweep_in, table, source,
    rhs, corr, last_corr, change,
    told, load_sem, halo_send, halo_recv, state_send, state_recv, relay_send, relay_recv, sweep_send, sweep_recv,
    rhs_send, rhs_recv, change_send, change_recv,
):
    me = lax.axis_index("inst")
    blk = lax.axis_index("blk")
    up, down = lax.rem(blk + 1, NB), lax.rem(blk + NB - 1, NB)
    my_core = lax.rem(me, 2)
    my_x = lax.rem(me // 2, 4)
    my_z = me // 8

    def peer(offset):
        z, x, c = offset
        return lax.rem(my_z + z, 2) * 8 + lax.rem(my_x + x, 4) * 2 + lax.rem(my_core + c, 2)

    relay_blk = lax.rem(blk + NB - 1 + 2 * my_z, NB)
    other_z = 1 - my_z

    barrier = pltpu.get_barrier_semaphore()
    partner = peer((0, 0, 1))
    for there in (up, down):
        t = 8 * my_z + 2 * my_x + 1
        pl.semaphore_signal(barrier, inc=1, device_id=(t, there), device_id_type=MESH)
    for offset in OFFSETS:
        t = peer(offset)

        @pl.when(lax.rem(t, 2) == 0)
        def _():
            pl.semaphore_signal(barrier, inc=1, device_id=(t, blk), device_id_type=MESH)

    @pl.when(my_core == 0)
    def _():
        pl.semaphore_signal(barrier, inc=1, device_id=(partner, blk), device_id_type=MESH)

    loads = [
        pltpu.make_async_copy(
            state_hbm.at[:, :, pl.ds(128 * zh, 128)], state.at[zh], load_sem.at[zh]
        )
        for zh in range(2)
    ]
    loads.append(pltpu.make_async_copy(multiples_hbm, multiples, load_sem.at[2]))
    for copy in loads:
        copy.start()
    for copy in loads:
        copy.wait()

    for y in range(8):
        for c in range(4):
            rows = pl.ds((c // 2) * 64 + y, 8, stride=8)
            s = [state[c % 2, v, rows, :] for v in range(5)]
            q = primitive(s)
            for v in range(5):
                cons[y + 4, v, c] = s[v]
                prim[y + 4, v, c] = q[v]
                row = (c // 2) * 640 + (y // 4) * 40 + v * 8 + (c % 2) * 4 + y % 4
                state_out[pl.ds(row, 8, stride=80), :] = s[v]

    def remote(source_ref, target_ref, send, recv, there):
        return pltpu.make_async_remote_copy(
            src_ref=source_ref, dst_ref=target_ref, send_sem=send, recv_sem=recv,
            device_id=there, device_id_type=MESH,
        )

    states = []
    for k, offset in enumerate(OFFSETS):
        t = peer(offset)
        first, rows = (0, 80) if offset[0] == 0 else (pl.multiple_of(40 * my_z, 8), 40)
        states.append(
            remote(
                state_out.at[pl.ds(pl.multiple_of(80 * t + first, 8), rows)],
                state_in.at[me, pl.ds(first, rows)],
                state_send.at[k], state_recv.at[k], (t, blk),
            )
        )
    own = state_out[pl.ds(pl.multiple_of(80 * me, 8), 80), :]
    state_in[me] = own

    def tell():
        pl.semaphore_signal(told, inc=1, device_id=(partner, blk), device_id_type=MESH)

    def send_states():
        for copy in states:
            copy.start()

    @pl.when(my_core == 0)
    def _():
        pl.semaphore_wait(barrier, NI - 1)
        tell()
        send_states()
        pl.semaphore_wait(told, 1)

    @pl.when(my_core == 1)
    def _():
        pl.semaphore_wait(told, 1)
        send_states()
        pl.semaphore_wait(barrier, 5)
        tell()

    halos = []
    for k, (mine, theirs, there) in enumerate(
        ((4, 12, down), (10, 2, up), (6, 14, down), (8, 0, up))
    ):
        halos.append(
            remote(
                cons.at[pl.ds(mine, 2)], cons.at[pl.ds(theirs, 2)],
                halo_send.at[k], halo_recv.at[k], (me, there),
            )
        )
        halos[-1].start()

    for k in range(8):
        rate = 0.0 if k == 0 else 0.5 * multiples[k - 1].astype(jnp.float32)
        rate = jnp.full((8, 128), rate, jnp.float32)
        det = 9.0 + rate * rate
        table[0, k] = 3.0 / det
        table[1, k] = rate / det
        table[2, k] = rate * 0.125

    def own_axial_radial(r, carry):
        axial_radial(prim, acc, r)
        return carry

    lax.fori_loop(4, 12, own_axial_radial, 0)

    def halo_primitive(r):
        for c in range(4):
            q = primitive([cons[r, v, c] for v in range(5)])
            for v in range(5):
                prim[r, v, c] = q[v]

    halos[0].wait_recv()
    halos[1].wait_recv()
    for r in (2, 3, 12, 13):
        halo_primitive(r)

    def segment(c):
        def emit(r, diff):
            s = [cons[r, v, c] - 0.025 * (acc[r, v, c] + diff[v]) for v in range(5)]
            q = primitive(s)
            for v in range(5):
                prim2[r, v, c] = q[v]

        return emit

    def own_column(c, carry):
        low, high = column(prim, c, 4, 11, segment(c))
        for v in range(5):
            edges[0, v, c] = low[v]
            edges[1, v, c] = high[v]
        return carry

    lax.fori_loop(0, 4, own_column, 0)

    def sweep2_axial_radial(r, carry):
        axial_radial(prim2, acc2, r)
        return carry

    def halo_axial_radial(k, carry):
        axial_radial(prim, acc, k + 2 + 8 * (k // 2))
        return carry

    lax.fori_loop(0, 4, halo_axial_radial, 0)
    lax.fori_loop(4, 12, sweep2_axial_radial, 0)

    halos[2].wait_recv()
    halos[3].wait_recv()
    for y in range(4):
        for v in range(5):
            for zh in range(2):
                relay_out[pl.ds(v * 8 + zh * 4 + y, 8, stride=40), :] = cons[
                    12 * my_z + y, v, 2 * other_z + zh
                ]
    for r in (0, 1, 14, 15):
        halo_primitive(r)

    def halo_column(c, carry):
        column(prim, c, 2, 3, segment(c), after=[edges[0, v, c] for v in range(5)])
        column(prim, c, 12, 13, segment(c), before=[edges[1, v, c] for v in range(5)])
        return carry

    lax.fori_loop(0, 4, halo_column, 0)

    def sweep2_column(c, carry):
        xh, zh = c // 2, lax.rem(c, 2)

        def emit(r, diff):
            for v in range(5):
                rows = pl.ds(xh * 640 + v * 16 + zh * 8 + (r - 4), 8, stride=80)
                sweep_out[rows, :] = acc2[r, v, c] + diff[v]

        column(prim2, c, 4, 11, emit)
        return carry

    lax.fori_loop(0, 4, sweep2_column, 0)

    sweeps = []
    for g, group in enumerate(GROUPS):
        first, rows = 16 * group[0], 16 * len(group)
        sweeps.append([])
        for k, offset in enumerate(OFFSETS):
            t = peer(offset)
            sweeps[g].append(
                remote(
                    sweep_out.at[pl.ds(pl.multiple_of(80 * t + first, 8), rows)],
                    sweep_in.at[me, pl.ds(first, rows)],
                    sweep_send.at[g, k], sweep_recv.at[g, k], (t, blk),
                )
            )
            sweeps[g][-1].start()
    own = sweep_out[pl.ds(pl.multiple_of(80 * me, 8), 80), :]
    sweep_in[me] = own

    relays = []
    for k, offset in enumerate(OFFSETS):
        if offset[0] == 1:
            t = peer(offset)
            relays.append(
                remote(
                    relay_out.at[pl.ds(pl.multiple_of(40 * (t - 8 * other_z), 8), 40)],
                    state_in.at[me, pl.ds(pl.multiple_of(40 * other_z, 8), 40)],
                    relay_send.at[k], relay_recv.at[k], (t, relay_blk),
                )
            )
            relays[-1].start()

    for copy in states + relays:
        copy.wait_recv()

    def solve(k, a, b):
        alpha, beta = table[0, k], table[1, k]
        return alpha * a - beta * b, alpha * b + beta * a

    def source_of(v, carry):
        for half in range(2):
            first = pl.multiple_of(v * 8 + half * 40, 8)
            x = forward([state_in[n, pl.ds(first, 8), :] for n in range(NI)])
            for k in range(1, 8):
                scale = table[2, k]
                a, b = solve(k, -(scale * x[2 * k + 1]), scale * x[2 * k])
                for zh in range(2):
                    rows = pl.ds(half * 4, 4)
                    source[v, zh, 2 * k, rows, :] = a[zh * 4 : zh * 4 + 4]
                    source[v, zh, 2 * k + 1, rows, :] = b[zh * 4 : zh * 4 + 4]
        return carry

    lax.fori_loop(0, 5, source_of, 0)

    rhs_copies = []
    for g, group in enumerate(GROUPS):
        for copy in sweeps[g]:
            copy.wait_recv()

        def right_hand(v, carry):
            for zh in range(2):
                first = pl.multiple_of(v * 16 + zh * 8, 8)
                x = forward([sweep_in[n, pl.ds(first, 8), :] for n in range(NI)])
                for k in range(8):
                    if k == 0:
                        a, b = x[0] * (-1.0 / 96.0), x[1] * (-1.0 / 96.0)
                    else:
                        a, b = solve(k, x[2 * k] * (-0.0625), x[2 * k + 1] * (-0.0625))
                        a = a + source[v, zh, 2 * k]
                        b = b + source[v, zh, 2 * k + 1]
                    rhs[v, zh, pl.ds(3 * 16 + k, 8, stride=16), :] = a
                    rhs[v, zh, pl.ds(3 * 16 + 8 + k, 8, stride=16), :] = b
            return carry

        lax.fori_loop(group[0], group[-1] + 1, right_hand, 0)
        vs = pl.ds(group[0], len(group))
        pair = []
        for k, (mine, theirs, there) in enumerate(((3, 11, down), (8, 0, up))):
            pair.append(
                remote(
                    rhs.at[vs, :, pl.ds(16 * mine, 48), :], rhs.at[vs, :, pl.ds(16 * theirs, 48), :],
                    rhs_send.at[g, k], rhs_recv.at[g, k], (me, there),
                )
            )
            pair[-1].start()
        rhs_copies.append(pair)

    pair_index = lax.broadcasted_iota(jnp.int32, (8, 128), 0)
    rate = jnp.zeros((8, 128), jnp.float32)
    for k in range(1, 8):
        rate = jnp.where(pair_index == k, 0.5 * multiples[k - 1].astype(jnp.float32), rate)
    det = 9.0 + rate * rate
    alpha, beta = 1.5 / det, (0.5 * rate) / det

    changes = []
    for g, group in enumerate(GROUPS):
        for copy in rhs_copies[g]:
            copy.wait_recv()

        def smooth(v, carry):
            def at(ref, row, ab, zh, shift=0):
                return ref[v, zh, pl.ds(16 * (row - shift) + 8 * ab, 8), :]

            def step(src, dst, first, last, src_shift=0, dst_shift=0):
                for row in range(first, last + 1):
                    nb = []
                    for ab in range(2):
                        lo, hi = (at(src, row, ab, zh, src_shift) for zh in range(2))
                        nlo, nhi = shift_next(lo, hi, 0.0, 1)
                        plo, phi = shift_prev(lo, hi, 0.0, 1)
                        both = []
                        for zh, t in ((0, nlo + plo), (1, nhi + phi)):
                            y = at(src, row - 1, ab, zh, src_shift) + at(src, row + 1, ab, zh, src_shift)
                            both.append(y + t)
                        nb.append(both)
                    for zh in range(2):
                        a, b = nb[0][zh], nb[1][zh]
                        for ab, t in ((0, alpha * a - beta * b), (1, alpha * b + beta * a)):
                            dst[v, zh, pl.ds(16 * (row - dst_shift) + 8 * ab, 8), :] = (
                                at(rhs, row, ab, zh) + t
                            )

            step(rhs, corr.at[0], 1, 12)
            step(corr.at[0], corr.at[1], 2, 11)
            step(corr.at[1], last_corr, 3, 10, 0, 3)
            for zh in range(2):
                c = [
                    last_corr[v, zh, pl.ds(8 * ab + k, 8, stride=16), :]
                    for k in range(8)
                    for ab in range(2)
                ]
                x = backward(c)
                for n in range(NI):
                    change[n, v, :, pl.ds(128 * zh, 128)] = x[n]
            return carry

        lax.fori_loop(group[0], group[-1] + 1, smooth, 0)
        vs = pl.ds(group[0], len(group))
        changes.append([])
        here = pl.ds(pl.multiple_of(8 * me, 8), 8)
        for k, offset in enumerate(OFFSETS):
            t = peer(offset)
            changes[g].append(
                remote(
                    change.at[t, vs], out.at[vs, here, :],
                    change_send.at[g, k], change_recv.at[g, k], (t, blk),
                )
            )
            changes[g][-1].start()
        for v in group:
            out[v, here, :] = change[me, v]

    for copies in [halos, states, relays] + sweeps + rhs_copies:
        for copy in copies:
            copy.wait_send()
    for copies in changes:
        for copy in copies:
            copy.wait()


def forward(x):
    e = [x[n] + x[n + 8] for n in range(8)]
    o = [x[n] - x[n + 8] for n in range(8)]
    ee = [e[n] + e[n + 4] for n in range(4)]
    eo = [e[n] - e[n + 4] for n in range(4)]
    out = [None] * 16
    s, t = ee[0] + ee[2], ee[1] + ee[3]
    out[0], out[1] = s + t, s - t
    out[8], out[9] = ee[0] - ee[2], ee[1] - ee[3]
    s, t = C2 * (eo[1] - eo[3]), C2 * (eo[1] + eo[3])
    out[4], out[5] = eo[0] + s, t + eo[2]
    out[12], out[13] = eo[0] - s, t - eo[2]
    p = [o[n] - o[8 - n] for n in range(1, 4)]
    q = [o[n] + o[8 - n] for n in range(1, 4)]
    m = C2 * p[1]
    s, t = o[0] + m, o[0] - m
    y, z = C1 * p[0] + C3 * p[2], C3 * p[0] - C1 * p[2]
    out[2], out[14] = s + y, s - y
    out[6], out[10] = t + z, t - z
    m = C2 * q[1]
    s, t = m + o[4], m - o[4]
    y, z = C3 * q[0] + C1 * q[2], C1 * q[0] - C3 * q[2]
    out[3], out[15] = y + s, y - s
    out[7], out[11] = z + t, z - t
    return out


def backward(c):
    s, t = c[0] + c[1], c[0] - c[1]
    ee = [s + c[8], t + c[9], s - c[8], t - c[9]]
    y, z = C2 * (c[4] - c[12]), C2 * (c[5] + c[13])
    eo = [c[4] + c[12], z + y, c[5] - c[13], z - y]
    e = [ee[n] + eo[n] for n in range(4)] + [ee[n] - eo[n] for n in range(4)]
    s, d = c[2] + c[14], c[2] - c[14]
    t, g = c[6] + c[10], c[6] - c[10]
    p = [None, C1 * d + C3 * g, C2 * (s - t), C3 * d - C1 * g]
    o0 = s + t
    s, d = c[3] + c[15], c[3] - c[15]
    t, g = c[7] + c[11], c[7] - c[11]
    q = [None, C3 * s + C1 * t, C2 * (d + g), C1 * s - C3 * t]
    o4 = d - g
    o = [o0] + [q[n] + p[n] for n in range(1, 4)] + [o4]
    o += [q[n] - p[n] for n in (3, 2, 1)]
    return [e[n] + o[n] for n in range(8)] + [e[n] - o[n] for n in range(8)]


def body(state, multiples):
    f32 = jnp.float32
    tiles = lambda rows: pltpu.VMEM((rows, 5, 4, 8, 128), f32)
    peers = len(OFFSETS)
    groups = len(GROUPS)
    dma = pltpu.SemaphoreType.DMA
    change = pl.pallas_call(
        kernel,
        out_shape=jax.ShapeDtypeStruct((5, 128, 256), f32),
        in_specs=[
            pl.BlockSpec(memory_space=pl.ANY),
            pl.BlockSpec(memory_space=pl.ANY),
        ],
        out_specs=pl.BlockSpec(memory_space=pltpu.VMEM),
        scratch_shapes=[
            pltpu.SMEM((7,), jnp.int32),
            pltpu.VMEM((2, 5, 128, 128), f32),
            tiles(16), tiles(16), tiles(16),
            pltpu.VMEM((2, 5, 4, 8, 128), f32),
            tiles(16), tiles(16),
            pltpu.VMEM((NI * 80, 128), f32),
            pltpu.VMEM((NI, 80, 128), f32),
            pltpu.VMEM((8 * 40, 128), f32),
            pltpu.VMEM((NI * 80, 128), f32),
            pltpu.VMEM((NI, 80, 128), f32),
            pltpu.VMEM((3, 8, 8, 128), f32),
            pltpu.VMEM((5, 2, 16, 8, 128), f32),
            pltpu.VMEM((5, 2, 14 * 16, 128), f32),
            pltpu.VMEM((2, 5, 2, 14 * 16, 128), f32),
            pltpu.VMEM((5, 2, 8 * 16, 128), f32),
            pltpu.VMEM((NI, 5, 8, 256), f32),
            pltpu.SemaphoreType.REGULAR,
            dma((3,)),
            dma((4,)), dma((4,)),
            dma((peers,)), dma((peers,)),
            dma((8,)), dma((8,)),
            dma((groups, peers)), dma((groups, peers)),
            dma((groups, 2)), dma((groups, 2)),
            dma((groups, peers)), dma((groups, peers)),
        ],
        compiler_params=pltpu.CompilerParams(
            collective_id=0, has_side_effects=True, vmem_limit_bytes=40 * 2**20
        ),
    )(multiples, state.reshape(5, 128, 256))
    return change.reshape(state.shape)


def solution(mesh):
    return jax.shard_map(
        body,
        mesh=mesh,
        in_specs=(P("inst", None, None, "blk", None), P()),
        out_specs=P("inst", None, None, "blk", None),
        check_vma=False,
    )
```
